32 devices in a mesh: dp: 4 (over y, x), blk: 8 (over z, core).
Axes of the slice: x: 2, y: 2, z: 4, core: 2. Of those that a mesh axis runs over, the one named last changes fastest.
Arguments:
- tokens: bfloat16 [1280, 3072], P(('dp', 'blk')), may hold values from -6 to 6
- expert_ids: int32 [1280, 2], P(('dp', 'blk')), may hold values from 0 to 7, as said below
- route_probs: float32 [1280, 2], P(('dp', 'blk')), may hold values from 0.2 to 1
- scale_exps: int32 [3], replicated, may hold values from -2 to 2
- w_gate: bfloat16 [3072, 8192], P(None, 'blk'), may hold values from -0.109375 to 0.109375
- w_up: bfloat16 [3072, 8192], P(None, 'blk'), may hold values from -0.109375 to 0.109375
- w_down: bfloat16 [8192, 3072], P('blk'), may hold values from -0.0625 to 0.0625
- out_grad: bfloat16 [1280, 3072], P(('dp', 'blk')), may hold values from -6 to 6
Outputs:
- mixed: bfloat16 [1280, 3072], P(('dp', 'blk'))
- input_grad: bfloat16 [1280, 3072], P(('dp', 'blk'))
- grad_gate: bfloat16 [3072, 8192], P('dp', 'blk')
- grad_up: bfloat16 [3072, 8192], P('dp', 'blk')
- grad_down: bfloat16 [8192, 3072], P('blk', 'dp')
The draws below stay inside these ranges and needn't reach their ends.
Inputs may be any that keep to these rules, and one draw needn't show every extreme that they name: `expert_ids`: the tokens are those dispatched to expert 0: each row names expert 0 and one other expert; the layer computes expert 0.
All inputs are finite; a program needn't handle non-finite values.
Results may differ from the reference program's by a relative error of at most 0.019.
Values may be sent and summed in bfloat16 or wider, within the bound.
A program may use at most 128 MiB of HBM per device.

```python
import jax
import jax.numpy as jnp

D = 3072
FF = 8192
EXPERTS = 8
TOP = 2
TOKENS = 1280


def draw_expert_ids(key, part):
    other_key = jax.random.fold_in(key, 11)
    place_key = jax.random.fold_in(key, 23)
    others = jax.random.randint(other_key, (TOKENS,), 1, EXPERTS, dtype=jnp.int32)
    others = others.at[0:EXPERTS - 1].set(jnp.arange(1, EXPERTS, dtype=jnp.int32))
    placed = jax.random.randint(place_key, (TOKENS,), 0, 2, dtype=jnp.int32)
    zeros = jnp.zeros((TOKENS,), jnp.int32)
    first = jnp.where(placed == 1, others, zeros)
    second = jnp.where(placed == 1, zeros, others)
    return jnp.stack([first, second], axis=1).astype(jnp.int32)


def with_spikes(array, key, source, target, shards_of, factor):
    def block_of(dim):
        return (jnp.arange(array.shape[dim]) // (array.shape[dim] // shards_of)).reshape((-1,) + (1,) * (array.ndim - 1 - dim))

    near = jax.random.permutation(key, shards_of)[block_of(target)]
    far = (block_of(target) + shards_of // 2) % shards_of
    return jnp.where((block_of(source) == near) | (block_of(source) == far), factor * array, array)


def levels(stream_key, extent, shards, low, top_value):
    loudness, own = 1.0, jax.random.fold_in(stream_key, 6)
    for axis_at, parts in shards:
        draws = jnp.exp(jax.random.uniform(jax.random.fold_in(own, axis_at), (parts,), jnp.float32, low / len(shards), top_value / len(shards)))
        loudness = loudness * jnp.repeat(draws, extent[axis_at] // parts).reshape([-1 if axis == axis_at else 1 for axis in range(len(extent))])
    return loudness


def bell_draw(own_key, shape, scale, limit, shards=(), held_as=jnp.bfloat16):
    level = levels(own_key, shape, shards, -0.22, 0.18) if shards else 1.0
    array = jax.random.normal(own_key, shape, jnp.float32) * scale * level
    return jnp.minimum(jnp.maximum(array, -limit), limit).astype(held_as)


def bell_draw_with(own_key, extent, width, bound, split, heavy, kind=jnp.bfloat16):
    array = width * jax.random.normal(own_key, extent, jnp.float32)
    if split:
        array = array * levels(own_key, extent, split, -0.22, 0.18)
    return jnp.clip(with_spikes(array, jax.random.fold_in(own_key, 3), *heavy), -bound, bound).astype(kind)


def setup_inputs(seed: int = 0) -> dict:
    seeds = jax.random.split(jax.random.key(seed), 9)
    tokens = bell_draw_with(seeds[0], (TOKENS, D), 1.0, 6.0, ((0, 32),), (0, 1, 32, 2.75))
    expert_ids = draw_expert_ids(jax.random.fold_in(seeds[8], 71), 0)
    route_probs = jnp.clip(0.2 + 0.8 * jax.random.uniform(seeds[2], (TOKENS, TOP), jnp.float32) ** levels(seeds[2], (TOKENS, TOP), ((0, 32),), -0.2, 0.2), 0.2, 1.0)
    scale_exps = jax.random.randint(seeds[3], (3,), -2, 3).astype(jnp.int32)
    w_gate = bell_draw(seeds[4], (D, FF), D ** -0.5, 0.109375, ((1, 8),))
    w_up = bell_draw(seeds[5], (D, FF), D ** -0.5, 0.109375, ((1, 8),))
    w_down = bell_draw(seeds[6], (FF, D), FF ** -0.5, 0.0625, ((0, 8),))
    out_grad = bell_draw_with(seeds[7], (TOKENS, D), 1.0, 6.0, ((0, 32),), (0, 1, 32, 2.75))
    return {"tokens": tokens, "expert_ids": expert_ids, "route_probs": route_probs, "scale_exps": scale_exps, "w_gate": w_gate, "w_up": w_up, "w_down": w_down, "out_grad": out_grad}


def reference(tokens, expert_ids, route_probs, scale_exps, w_gate, w_up, w_down, out_grad):
    scales = jnp.exp2(scale_exps.astype(jnp.float32))
    combine = jnp.sum(jnp.where(expert_ids == 0, route_probs, jnp.zeros_like(route_probs)), axis=1)[:, None]
    gate_pre = jnp.dot(tokens, w_gate, preferred_element_type=jnp.float32) * scales[0]
    up_pre = jnp.dot(tokens, w_up, preferred_element_type=jnp.float32) * scales[1]
    sigmoid_gate = jax.nn.sigmoid(gate_pre)
    hidden = (gate_pre * sigmoid_gate * up_pre).astype(jnp.bfloat16)
    expert_out = jnp.dot(hidden, w_down, preferred_element_type=jnp.float32) * scales[2]
    mixed = (combine * expert_out).astype(jnp.bfloat16)
    scaled = (combine * out_grad.astype(jnp.float32)).astype(jnp.bfloat16)
    d_hidden = jnp.dot(scaled, w_down.T, preferred_element_type=jnp.float32) * scales[2]
    d_gate = (d_hidden * up_pre * sigmoid_gate * (1.0 + gate_pre * (1.0 - sigmoid_gate))).astype(jnp.bfloat16)
    d_up = (d_hidden * gate_pre * sigmoid_gate).astype(jnp.bfloat16)
    input_grad = (jnp.dot(d_gate, w_gate.T, preferred_element_type=jnp.float32) * scales[0]
                  + jnp.dot(d_up, w_up.T, preferred_element_type=jnp.float32) * scales[1]).astype(jnp.bfloat16)
    grad_gate = (jnp.dot(tokens.T, d_gate, preferred_element_type=jnp.float32) * scales[0]).astype(jnp.bfloat16)
    grad_up = (jnp.dot(tokens.T, d_up, preferred_element_type=jnp.float32) * scales[1]).astype(jnp.bfloat16)
    grad_down = (jnp.dot(hidden.T, scaled, preferred_element_type=jnp.float32) * scales[2]).astype(jnp.bfloat16)
    return (mixed, input_grad, grad_gate, grad_up, grad_down)
```

```python
import jax
import jax.numpy as jnp
from jax import lax
from jax.sharding import PartitionSpec as P


def contract_rows(left, right):
    return lax.dot_general(
        left, right, (((0,), (0,)), ((), ())), preferred_element_type=jnp.float32
    )


def contract_cols(left, right):
    return lax.dot_general(
        left, right, (((1,), (1,)), ((), ())), preferred_element_type=jnp.float32
    )


def local(tokens, expert_ids, route_probs, scale_exps, w_gate, w_up, w_down, out_grad):
    scales = jnp.exp2(scale_exps.astype(jnp.float32))
    combine = jnp.sum(jnp.where(expert_ids == 0, route_probs, jnp.zeros_like(route_probs)), axis=1)[
        :, None
    ]
    gathered = lax.all_gather(tokens, "blk", axis=0, tiled=True)
    gate_pre = jnp.dot(gathered, w_gate, preferred_element_type=jnp.float32) * scales[0]
    up_pre = jnp.dot(gathered, w_up, preferred_element_type=jnp.float32) * scales[1]
    sigmoid_gate = jax.nn.sigmoid(gate_pre)
    hidden = (gate_pre * sigmoid_gate * up_pre).astype(jnp.bfloat16)
    expert_out = lax.psum_scatter(
        (jnp.dot(hidden, w_down, preferred_element_type=jnp.float32) * scales[2]).astype(
            jnp.bfloat16
        ),
        "blk",
        scatter_dimension=0,
        tiled=True,
    ).astype(jnp.float32)
    mixed = (combine * expert_out).astype(jnp.bfloat16)
    scaled = (combine * out_grad.astype(jnp.float32)).astype(jnp.bfloat16)
    scaled_all = lax.all_gather(scaled, "blk", axis=0, tiled=True)
    d_hidden = contract_cols(scaled_all, w_down) * scales[2]
    d_gate = (d_hidden * up_pre * sigmoid_gate * (1.0 + gate_pre * (1.0 - sigmoid_gate))).astype(
        jnp.bfloat16
    )
    d_up = (d_hidden * gate_pre * sigmoid_gate).astype(jnp.bfloat16)
    input_grad = lax.psum_scatter(
        (contract_cols(d_gate, w_gate) * scales[0] + contract_cols(d_up, w_up) * scales[1]).astype(
            jnp.bfloat16
        ),
        "blk",
        scatter_dimension=0,
        tiled=True,
    )
    tokens_slice = lax.all_to_all(gathered, "dp", split_axis=1, concat_axis=0, tiled=True)
    scaled_slice = lax.all_to_all(scaled_all, "dp", split_axis=1, concat_axis=0, tiled=True)
    hidden_all = lax.all_gather(hidden, "dp", axis=0, tiled=True)
    d_gate_all = lax.all_gather(d_gate, "dp", axis=0, tiled=True)
    d_up_all = lax.all_gather(d_up, "dp", axis=0, tiled=True)
    grad_gate = contract_rows(tokens_slice, d_gate_all) * scales[0]
    grad_up = contract_rows(tokens_slice, d_up_all) * scales[1]
    grad_down = contract_rows(hidden_all, scaled_slice) * scales[2]
    return (
        mixed,
        input_grad,
        grad_gate.astype(jnp.bfloat16),
        grad_up.astype(jnp.bfloat16),
        grad_down.astype(jnp.bfloat16),
    )


def solution(mesh):
    return jax.shard_map(
        local,
        mesh=mesh,
        in_specs=(
            P(("dp", "blk"), None),
            P(("dp", "blk"), None),
            P(("dp", "blk"), None),
            P(),
            P(None, "blk"),
            P(None, "blk"),
            P("blk", None),
            P(("dp", "blk"), None),
        ),
        out_specs=(
            P(("dp", "blk"), None),
            P(("dp", "blk"), None),
            P("dp", "blk"),
            P("dp", "blk"),
            P("blk", "dp"),
        ),
        check_vma=False,
    )
```

```python
import functools

import jax
import jax.numpy as jnp
from jax import lax
from jax.experimental import pallas as pl
from jax.experimental.pallas import tpu as pltpu
from jax.sharding import PartitionSpec as P


def contract_rows(left, right):
    return lax.dot_general(
        left, right, (((0,), (0,)), ((), ())), preferred_element_type=jnp.float32
    )


def contract_cols(left, right):
    return lax.dot_general(
        left, right, (((1,), (1,)), ((), ())), preferred_element_type=jnp.float32
    )


MESH = pl.DeviceIdType.MESH


def exchange_kernel(
    n, tok, sca, hid, dg, du, _out_part, _in_part, tok_o, sca_o, hid_o, dg_o, du_o, send, recv, fsend, frecv, own
):
    me = lax.axis_index("dp")
    blk = lax.axis_index("blk")
    core = blk % 2
    sibling = blk + 1 - 2 * core
    rows = hid.shape[0]
    half = rows // 2
    width = tok_o.shape[2]
    my_half = pl.ds(pl.multiple_of(core * half, 16), half)

    barrier = pltpu.get_barrier_semaphore()
    for j in range(1, n):
        pl.semaphore_signal(
            barrier, inc=1, device_id=((me + j) % n, blk), device_id_type=MESH
        )
    pl.semaphore_signal(barrier, inc=1, device_id=(me, sibling), device_id_type=MESH)
    pl.semaphore_wait(barrier, n)

    def columns(p):
        return pl.ds(pl.multiple_of(p * width, 128), width)

    slices = ((tok, tok_o), (sca, sca_o))
    wholes = ((hid, hid_o), (dg, dg_o), (du, du_o))
    sliced, sent, local = [], [], []
    for a, (src, dst) in enumerate(slices):
        for j in range(1, n):
            p = (me + j) % n
            copy = pltpu.make_async_remote_copy(
                src_ref=src.at[my_half, columns(p)],
                dst_ref=dst.at[me, my_half],
                send_sem=send.at[a, j],
                recv_sem=recv.at[a, j],
                device_id=(p, blk),
                device_id_type=MESH,
            )
            copy.start()
            sliced.append((a, j, dst, copy))
    for a, (src, dst) in enumerate(wholes):
        for j in range(1, n):
            p = (me + j) % n
            copy = pltpu.make_async_remote_copy(
                src_ref=src,
                dst_ref=dst.at[me],
                send_sem=send.at[2 + a, j],
                recv_sem=recv.at[2 + a, j],
                device_id=(p, blk),
                device_id_type=MESH,
            )
            copy.start()
            sent.append(copy)
    for a, (src, dst) in enumerate(slices):
        copy = pltpu.make_async_copy(src.at[:, columns(me)], dst.at[me], own.at[a])
        copy.start()
        local.append(copy)
    for a, (src, dst) in enumerate(wholes):
        copy = pltpu.make_async_copy(src, dst.at[me], own.at[2 + a])
        copy.start()
        local.append(copy)
    forwards = []
    for a, j, dst, copy in sliced:
        copy.wait_recv()
        landed = dst.at[(me + n - j) % n, my_half]
        forward = pltpu.make_async_remote_copy(
            src_ref=landed,
            dst_ref=landed,
            send_sem=fsend.at[a, j],
            recv_sem=frecv.at[a, j],
            device_id=(me, sibling),
            device_id_type=MESH,
        )
        forward.start()
        forwards.append(forward)
    for _, _, _, copy in sliced:
        copy.wait_send()
    for copy in forwards + sent + local:
        copy.wait()


def exchange(n, tokens, scaled, hidden, d_gate, d_up, out_part, in_part):
    rows, features = tokens.shape
    units = hidden.shape[1]
    part = jax.ShapeDtypeStruct((n, rows, features // n), jnp.bfloat16)
    whole = jax.ShapeDtypeStruct((n, rows, units), jnp.bfloat16)
    outs = pl.pallas_call(
        functools.partial(exchange_kernel, n),
        out_shape=(part, part, whole, whole, whole),
        in_specs=[pl.BlockSpec(memory_space=pl.ANY)] * 7,
        out_specs=[pl.BlockSpec(memory_space=pl.ANY)] * 5,
        scratch_shapes=[
            pltpu.SemaphoreType.DMA((5, n)),
            pltpu.SemaphoreType.DMA((5, n)),
            pltpu.SemaphoreType.DMA((2, n)),
            pltpu.SemaphoreType.DMA((2, n)),
            pltpu.SemaphoreType.DMA((5,)),
        ],
        compiler_params=pltpu.CompilerParams(collective_id=0, has_side_effects=True),
        cost_estimate=pl.CostEstimate(flops=0, bytes_accessed=300_000_000, transcendentals=0),
    )(tokens, scaled, hidden, d_gate, d_up, out_part, in_part)
    return [out.reshape(n * rows, out.shape[2]) for out in outs]


def local(n, tokens, expert_ids, route_probs, scale_exps, w_gate, w_up, w_down, out_grad):
    scales = jnp.exp2(scale_exps.astype(jnp.float32))
    combine = jnp.sum(jnp.where(expert_ids == 0, route_probs, jnp.zeros_like(route_probs)), axis=1)[
        :, None
    ]
    gathered = lax.all_gather(tokens, "blk", axis=0, tiled=True)
    gate_pre = jnp.dot(gathered, w_gate, preferred_element_type=jnp.float32) * scales[0]
    up_pre = jnp.dot(gathered, w_up, preferred_element_type=jnp.float32) * scales[1]
    sigmoid_gate = jax.nn.sigmoid(gate_pre)
    hidden = (gate_pre * sigmoid_gate * up_pre).astype(jnp.bfloat16)
    out_part = (jnp.dot(hidden, w_down, preferred_element_type=jnp.float32) * scales[2]).astype(
        jnp.bfloat16
    )
    scaled = (combine * out_grad.astype(jnp.float32)).astype(jnp.bfloat16)
    scaled_all = lax.all_gather(scaled, "blk", axis=0, tiled=True)
    d_hidden = contract_cols(scaled_all, w_down) * scales[2]
    d_gate = (d_hidden * up_pre * sigmoid_gate * (1.0 + gate_pre * (1.0 - sigmoid_gate))).astype(
        jnp.bfloat16
    )
    d_up = (d_hidden * gate_pre * sigmoid_gate).astype(jnp.bfloat16)
    in_part = (
        contract_cols(d_gate, w_gate) * scales[0] + contract_cols(d_up, w_up) * scales[1]
    ).astype(jnp.bfloat16)
    expert_out = lax.psum_scatter(out_part, "blk", scatter_dimension=0, tiled=True)
    mixed = (combine * expert_out.astype(jnp.float32)).astype(jnp.bfloat16)
    input_grad = lax.psum_scatter(in_part, "blk", scatter_dimension=0, tiled=True)
    tokens_slice, scaled_slice, hidden_all, d_gate_all, d_up_all = exchange(
        n, gathered, scaled_all, hidden, d_gate, d_up, out_part, in_part
    )
    grad_gate = contract_rows(tokens_slice, d_gate_all) * scales[0]
    grad_up = contract_rows(tokens_slice, d_up_all) * scales[1]
    grad_down = contract_rows(hidden_all, scaled_slice) * scales[2]
    return (
        mixed,
        input_grad,
        grad_gate.astype(jnp.bfloat16),
        grad_up.astype(jnp.bfloat16),
        grad_down.astype(jnp.bfloat16),
    )


def solution(mesh):
    return jax.shard_map(
        functools.partial(local, mesh.shape["dp"]),
        mesh=mesh,
        in_specs=(
            P(("dp", "blk"), None),
            P(("dp", "blk"), None),
            P(("dp", "blk"), None),
            P(),
            P(None, "blk"),
            P(None, "blk"),
            P("blk", None),
            P(("dp", "blk"), None),
        ),
        out_specs=(
            P(("dp", "blk"), None),
            P(("dp", "blk"), None),
            P("dp", "blk"),
            P("dp", "blk"),
            P("blk", "dp"),
        ),
        check_vma=False,
    )
```

```python
import functools

import jax
import jax.numpy as jnp
from jax import lax
from jax.experimental import pallas as pl
from jax.experimental.pallas import tpu as pltpu
from jax.sharding import PartitionSpec as P


def contract_rows(left, right):
    return lax.dot_general(
        left, right, (((0,), (0,)), ((), ())), preferred_element_type=jnp.float32
    )


def contract_cols(left, right):
    return lax.dot_general(
        left, right, (((1,), (1,)), ((), ())), preferred_element_type=jnp.float32
    )


MESH = pl.DeviceIdType.MESH


def exchange_kernel(
    n, tok, sca, hid, dg, du, _out_part, _in_part, tok_o, sca_o, hid_o, dg_o, du_o, send, recv, fsend, frecv, own
):
    me = lax.axis_index("dp")
    blk = lax.axis_index("blk")
    core = blk % 2
    sibling = blk + 1 - 2 * core
    rows = hid.shape[0]
    half = rows // 2
    width = tok_o.shape[2]
    my_half = pl.ds(pl.multiple_of(core * half, 16), half)

    barrier = pltpu.get_barrier_semaphore()
    for j in range(1, n):
        pl.semaphore_signal(
            barrier, inc=1, device_id=((me + j) % n, blk), device_id_type=MESH
        )
    pl.semaphore_signal(barrier, inc=1, device_id=(me, sibling), device_id_type=MESH)
    pl.semaphore_wait(barrier, n)

    def columns(p):
        return pl.ds(pl.multiple_of(p * width, 128), width)

    slices = ((tok, tok_o), (sca, sca_o))
    wholes = ((hid, hid_o), (dg, dg_o), (du, du_o))
    sliced, sent, local = [], [], []
    for a, (src, dst) in enumerate(slices):
        for j in range(1, n):
            p = (me + j) % n
            copy = pltpu.make_async_remote_copy(
                src_ref=src.at[my_half, columns(p)],
                dst_ref=dst.at[me, my_half],
                send_sem=send.at[a, j],
                recv_sem=recv.at[a, j],
                device_id=(p, blk),
                device_id_type=MESH,
            )
            copy.start()
            sliced.append((a, j, dst, copy))
    across, along = me + 1 - 2 * (me % 2), (me + 2) % n
    passed = []
    for a, (src, dst) in enumerate(wholes):
        for j in range(1, 3 if n == 4 else n):
            p = (me + j) % n
            if n == 4:
                p = across if j == 1 else along
            copy = pltpu.make_async_remote_copy(
                src_ref=src,
                dst_ref=dst.at[me],
                send_sem=send.at[2 + a, j],
                recv_sem=recv.at[2 + a, j],
                device_id=(p, blk),
                device_id_type=MESH,
            )
            copy.start()
            (passed if n == 4 else sent).append((a, j, dst, copy))
    for a, (src, dst) in enumerate(slices):
        copy = pltpu.make_async_copy(src.at[:, columns(me)], dst.at[me], own.at[a])
        copy.start()
        local.append(copy)
    for a, (src, dst) in enumerate(wholes):
        copy = pltpu.make_async_copy(src, dst.at[me], own.at[2 + a])
        copy.start()
        local.append(copy)
    forwards = []
    for a, j, dst, copy in sliced:
        copy.wait_recv()
        landed = dst.at[(me + n - j) % n, my_half]
        forward = pltpu.make_async_remote_copy(
            src_ref=landed,
            dst_ref=landed,
            send_sem=fsend.at[a, j],
            recv_sem=frecv.at[a, j],
            device_id=(me, sibling),
            device_id_type=MESH,
        )
        forward.start()
        forwards.append(forward)
    for a, j, dst, copy in passed:
        copy.wait_recv()
        owner, target = (across, along) if j == 1 else (along, across)
        landed = dst.at[owner, pl.ds((j - 1) * half, half)]
        forward = pltpu.make_async_remote_copy(
            src_ref=landed,
            dst_ref=landed,
            send_sem=fsend.at[2 + a, j],
            recv_sem=frecv.at[2 + a, j],
            device_id=(target, blk),
            device_id_type=MESH,
        )
        forward.start()
        forwards.append(forward)
    for _, _, _, copy in sliced + passed:
        copy.wait_send()
    for copy in forwards + [copy for _, _, _, copy in sent] + local:
        copy.wait()


def exchange(n, tokens, scaled, hidden, d_gate, d_up, out_part, in_part):
    rows, features = tokens.shape
    units = hidden.shape[1]
    part = jax.ShapeDtypeStruct((n, rows, features // n), jnp.bfloat16)
    whole = jax.ShapeDtypeStruct((n, rows, units), jnp.bfloat16)
    outs = pl.pallas_call(
        functools.partial(exchange_kernel, n),
        out_shape=(part, part, whole, whole, whole),
        in_specs=[pl.BlockSpec(memory_space=pl.ANY)] * 7,
        out_specs=[pl.BlockSpec(memory_space=pl.ANY)] * 5,
        scratch_shapes=[
            pltpu.SemaphoreType.DMA((5, n)),
            pltpu.SemaphoreType.DMA((5, n)),
            pltpu.SemaphoreType.DMA((5, n)),
            pltpu.SemaphoreType.DMA((5, n)),
            pltpu.SemaphoreType.DMA((5,)),
        ],
        compiler_params=pltpu.CompilerParams(collective_id=0, has_side_effects=True),
        cost_estimate=pl.CostEstimate(flops=0, bytes_accessed=300_000_000, transcendentals=0),
    )(tokens, scaled, hidden, d_gate, d_up, out_part, in_part)
    return [out.reshape(n * rows, out.shape[2]) for out in outs]


def local(n, tokens, expert_ids, route_probs, scale_exps, w_gate, w_up, w_down, out_grad):
    scales = jnp.exp2(scale_exps.astype(jnp.float32))
    combine = jnp.sum(jnp.where(expert_ids == 0, route_probs, jnp.zeros_like(route_probs)), axis=1)[
        :, None
    ]
    gathered = lax.all_gather(tokens, "blk", axis=0, tiled=True)
    gate_pre = jnp.dot(gathered, w_gate, preferred_element_type=jnp.float32) * scales[0]
    up_pre = jnp.dot(gathered, w_up, preferred_element_type=jnp.float32) * scales[1]
    sigmoid_gate = jax.nn.sigmoid(gate_pre)
    hidden = (gate_pre * sigmoid_gate * up_pre).astype(jnp.bfloat16)
    out_part = (jnp.dot(hidden, w_down, preferred_element_type=jnp.float32) * scales[2]).astype(
        jnp.bfloat16
    )
    scaled = (combine * out_grad.astype(jnp.float32)).astype(jnp.bfloat16)
    scaled_all = lax.all_gather(scaled, "blk", axis=0, tiled=True)
    d_hidden = contract_cols(scaled_all, w_down) * scales[2]
    d_gate = (d_hidden * up_pre * sigmoid_gate * (1.0 + gate_pre * (1.0 - sigmoid_gate))).astype(
        jnp.bfloat16
    )
    d_up = (d_hidden * gate_pre * sigmoid_gate).astype(jnp.bfloat16)
    in_part = (
        contract_cols(d_gate, w_gate) * scales[0] + contract_cols(d_up, w_up) * scales[1]
    ).astype(jnp.bfloat16)
    expert_out = lax.psum_scatter(out_part, "blk", scatter_dimension=0, tiled=True)
    mixed = (combine * expert_out.astype(jnp.float32)).astype(jnp.bfloat16)
    input_grad = lax.psum_scatter(in_part, "blk", scatter_dimension=0, tiled=True)
    tokens_slice, scaled_slice, hidden_all, d_gate_all, d_up_all = exchange(
        n, gathered, scaled_all, hidden, d_gate, d_up, out_part, in_part
    )
    grad_gate = contract_rows(tokens_slice, d_gate_all) * scales[0]
    grad_up = contract_rows(tokens_slice, d_up_all) * scales[1]
    grad_down = contract_rows(hidden_all, scaled_slice) * scales[2]
    return (
        mixed,
        input_grad,
        grad_gate.astype(jnp.bfloat16),
        grad_up.astype(jnp.bfloat16),
        grad_down.astype(jnp.bfloat16),
    )


def solution(mesh):
    return jax.shard_map(
        functools.partial(local, mesh.shape["dp"]),
        mesh=mesh,
        in_specs=(
            P(("dp", "blk"), None),
            P(("dp", "blk"), None),
            P(("dp", "blk"), None),
            P(),
            P(None, "blk"),
            P(None, "blk"),
            P("blk", None),
            P(("dp", "blk"), None),
        ),
        out_specs=(
            P(("dp", "blk"), None),
            P(("dp", "blk"), None),
            P("dp", "blk"),
            P("dp", "blk"),
            P("blk", "dp"),
        ),
        check_vma=False,
    )
```

```python
import functools

import jax
import jax.numpy as jnp
from jax import lax
from jax.experimental import pallas as pl
from jax.experimental.pallas import tpu as pltpu
from jax.sharding import PartitionSpec as P


def contract_rows(left, right):
    return lax.dot_general(
        left, right, (((0,), (0,)), ((), ())), preferred_element_type=jnp.float32
    )


def contract_cols(left, right):
    return lax.dot_general(
        left, right, (((1,), (1,)), ((), ())), preferred_element_type=jnp.float32
    )


MESH = pl.DeviceIdType.MESH


def exchange_kernel(n, n_slices, n_wholes, n_order, *refs):
    total = n_slices + n_wholes
    ins, outs = refs[:total], refs[total + n_order : 2 * total + n_order]
    send, recv, fsend, frecv, own = refs[-5:]
    slices = tuple(zip(ins[:n_slices], outs[:n_slices]))
    wholes = tuple(zip(ins[n_slices:], outs[n_slices:]))
    me = lax.axis_index("dp")
    blk = lax.axis_index("blk")
    core = blk % 2
    sibling = blk + 1 - 2 * core
    rows = ins[0].shape[0]
    half = rows // 2
    width = outs[0].shape[2]
    my_half = pl.ds(pl.multiple_of(core * half, 16), half)

    barrier = pltpu.get_barrier_semaphore()
    for j in range(1, n):
        pl.semaphore_signal(
            barrier, inc=1, device_id=((me + j) % n, blk), device_id_type=MESH
        )
    pl.semaphore_signal(barrier, inc=1, device_id=(me, sibling), device_id_type=MESH)
    pl.semaphore_wait(barrier, n)

    def columns(p):
        return pl.ds(pl.multiple_of(p * width, 128), width)

    sliced, sent, local = [], [], []
    for a, (src, dst) in enumerate(slices):
        for j in range(1, n):
            p = (me + j) % n
            copy = pltpu.make_async_remote_copy(
                src_ref=src.at[my_half, columns(p)],
                dst_ref=dst.at[me, my_half],
                send_sem=send.at[a, j],
                recv_sem=recv.at[a, j],
                device_id=(p, blk),
                device_id_type=MESH,
            )
            copy.start()
            sliced.append((a, j, dst, copy))
    across, along = me + 1 - 2 * (me % 2), (me + 2) % n
    passed = []
    for a, (src, dst) in enumerate(wholes):
        for j in range(1, 3 if n == 4 else n):
            p = (me + j) % n
            if n == 4:
                p = across if j == 1 else along
            copy = pltpu.make_async_remote_copy(
                src_ref=src,
                dst_ref=dst.at[me],
                send_sem=send.at[n_slices + a, j],
                recv_sem=recv.at[n_slices + a, j],
                device_id=(p, blk),
                device_id_type=MESH,
            )
            copy.start()
            (passed if n == 4 else sent).append((a, j, dst, copy))
    for a, (src, dst) in enumerate(slices):
        copy = pltpu.make_async_copy(src.at[:, columns(me)], dst.at[me], own.at[a])
        copy.start()
        local.append(copy)
    for a, (src, dst) in enumerate(wholes):
        copy = pltpu.make_async_copy(src, dst.at[me], own.at[n_slices + a])
        copy.start()
        local.append(copy)
    forwards = []
    for a, j, dst, copy in sliced:
        copy.wait_recv()
        landed = dst.at[(me + n - j) % n, my_half]
        forward = pltpu.make_async_remote_copy(
            src_ref=landed,
            dst_ref=landed,
            send_sem=fsend.at[a, j],
            recv_sem=frecv.at[a, j],
            device_id=(me, sibling),
            device_id_type=MESH,
        )
        forward.start()
        forwards.append(forward)
    for a, j, dst, copy in passed:
        copy.wait_recv()
        owner, target = (across, along) if j == 1 else (along, across)
        landed = dst.at[owner, pl.ds((j - 1) * half, half)]
        forward = pltpu.make_async_remote_copy(
            src_ref=landed,
            dst_ref=landed,
            send_sem=fsend.at[n_slices + a, j],
            recv_sem=frecv.at[n_slices + a, j],
            device_id=(target, blk),
            device_id_type=MESH,
        )
        forward.start()
        forwards.append(forward)
    for _, _, _, copy in sliced + passed:
        copy.wait_send()
    for copy in forwards + [copy for _, _, _, copy in sent] + local:
        copy.wait()


def exchange(n, slices, wholes, order, collective_id, cost, through=False):
    total = len(slices) + len(wholes)
    out_shape = [
        jax.ShapeDtypeStruct((n, x.shape[0], x.shape[1] // n), jnp.bfloat16) for x in slices
    ] + [jax.ShapeDtypeStruct((n,) + x.shape, jnp.bfloat16) for x in wholes]
    if through:
        out_shape.append(jax.ShapeDtypeStruct(slices[0].shape, jnp.bfloat16))
    outs = pl.pallas_call(
        functools.partial(exchange_kernel, n, len(slices), len(wholes), len(order)),
        out_shape=out_shape,
        in_specs=[pl.BlockSpec(memory_space=pl.ANY)] * (total + len(order)),
        out_specs=[pl.BlockSpec(memory_space=pl.ANY)] * len(out_shape),
        input_output_aliases={0: total} if through else {},
        scratch_shapes=[pltpu.SemaphoreType.DMA((total, n))] * 4
        + [pltpu.SemaphoreType.DMA((total,))],
        compiler_params=pltpu.CompilerParams(
            collective_id=collective_id, has_side_effects=True
        ),
        cost_estimate=pl.CostEstimate(flops=0, bytes_accessed=cost, transcendentals=0),
    )(*slices, *wholes, *order)
    return [out.reshape(n * out.shape[1], out.shape[2]) for out in outs[:total]] + list(outs[total:])


def local(n, tokens, expert_ids, route_probs, scale_exps, w_gate, w_up, w_down, out_grad):
    scales = jnp.exp2(scale_exps.astype(jnp.float32))
    combine = jnp.sum(jnp.where(expert_ids == 0, route_probs, jnp.zeros_like(route_probs)), axis=1)[
        :, None
    ]
    gathered = lax.all_gather(tokens, "blk", axis=0, tiled=True)
    gate_pre = jnp.dot(gathered, w_gate, preferred_element_type=jnp.float32) * scales[0]
    up_pre = jnp.dot(gathered, w_up, preferred_element_type=jnp.float32) * scales[1]
    sigmoid_gate = jax.nn.sigmoid(gate_pre)
    hidden = (gate_pre * sigmoid_gate * up_pre).astype(jnp.bfloat16)
    out_part = (jnp.dot(hidden, w_down, preferred_element_type=jnp.float32) * scales[2]).astype(
        jnp.bfloat16
    )
    scaled = (combine * out_grad.astype(jnp.float32)).astype(jnp.bfloat16)
    scaled_all = lax.all_gather(scaled, "blk", axis=0, tiled=True)
    scaled_slice, scaled_all = exchange(n, [scaled_all], [], [], 1, 45_000_000, through=True)
    d_hidden = contract_cols(scaled_all, w_down) * scales[2]
    d_gate = (d_hidden * up_pre * sigmoid_gate * (1.0 + gate_pre * (1.0 - sigmoid_gate))).astype(
        jnp.bfloat16
    )
    d_up = (d_hidden * gate_pre * sigmoid_gate).astype(jnp.bfloat16)
    in_part = (
        contract_cols(d_gate, w_gate) * scales[0] + contract_cols(d_up, w_up) * scales[1]
    ).astype(jnp.bfloat16)
    expert_out = lax.psum_scatter(out_part, "blk", scatter_dimension=0, tiled=True)
    mixed = (combine * expert_out.astype(jnp.float32)).astype(jnp.bfloat16)
    input_grad = lax.psum_scatter(in_part, "blk", scatter_dimension=0, tiled=True)
    tokens_slice, hidden_all, d_gate_all, d_up_all = exchange(
        n, [gathered], [hidden, d_gate, d_up], [out_part, in_part, scaled_slice], 0, 300_000_000
    )
    grad_gate = contract_rows(tokens_slice, d_gate_all) * scales[0]
    grad_up = contract_rows(tokens_slice, d_up_all) * scales[1]
    grad_down = contract_rows(hidden_all, scaled_slice) * scales[2]
    return (
        mixed,
        input_grad,
        grad_gate.astype(jnp.bfloat16),
        grad_up.astype(jnp.bfloat16),
        grad_down.astype(jnp.bfloat16),
    )


def solution(mesh):
    return jax.shard_map(
        functools.partial(local, mesh.shape["dp"]),
        mesh=mesh,
        in_specs=(
            P(("dp", "blk"), None),
            P(("dp", "blk"), None),
            P(("dp", "blk"), None),
            P(),
            P(None, "blk"),
            P(None, "blk"),
            P("blk", None),
            P(("dp", "blk"), None),
        ),
        out_specs=(
            P(("dp", "blk"), None),
            P(("dp", "blk"), None),
            P("dp", "blk"),
            P("dp", "blk"),
            P("blk", "dp"),
        ),
        check_vma=False,
    )
```

```python
import functools

import jax
import jax.numpy as jnp
from jax import lax
from jax.experimental import pallas as pl
from jax.experimental.pallas import tpu as pltpu
from jax.sharding import PartitionSpec as P


def contract_rows(left, right):
    return lax.dot_general(
        left, right, (((0,), (0,)), ((), ())), preferred_element_type=jnp.float32
    )


def contract_cols(left, right):
    return lax.dot_general(
        left, right, (((1,), (1,)), ((), ())), preferred_element_type=jnp.float32
    )


MESH = pl.DeviceIdType.MESH


def exchange_kernel(n, n_slices, n_wholes, n_order, *refs):
    total = n_slices + n_wholes
    ins, outs = refs[:total], refs[total + n_order : 2 * total + n_order]
    send, recv, fsend, frecv, own = refs[-5:]
    slices = tuple(zip(ins[:n_slices], outs[:n_slices]))
    wholes = tuple(zip(ins[n_slices:], outs[n_slices:]))
    me = lax.axis_index("dp")
    blk = lax.axis_index("blk")
    core = blk % 2
    sibling = blk + 1 - 2 * core
    rows = ins[0].shape[0]
    half = rows // 2
    width = outs[0].shape[2]
    my_half = pl.ds(pl.multiple_of(core * half, 16), half)

    barrier = pltpu.get_barrier_semaphore()
    for j in range(1, n):
        pl.semaphore_signal(
            barrier, inc=1, device_id=((me + j) % n, blk), device_id_type=MESH
        )
    pl.semaphore_signal(barrier, inc=1, device_id=(me, sibling), device_id_type=MESH)
    pl.semaphore_wait(barrier, n)

    def columns(p):
        return pl.ds(pl.multiple_of(p * width, 128), width)

    sliced, sent, local = [], [], []
    across, along = me + 1 - 2 * (me % 2), (me + 2) % n
    passed = []
    for a, (src, dst) in enumerate(wholes):
        for j in range(1, 3 if n == 4 else n):
            p = (me + j) % n
            if n == 4:
                p = across if j == 1 else along
            copy = pltpu.make_async_remote_copy(
                src_ref=src,
                dst_ref=dst.at[me],
                send_sem=send.at[n_slices + a, j],
                recv_sem=recv.at[n_slices + a, j],
                device_id=(p, blk),
                device_id_type=MESH,
            )
            copy.start()
            (passed if n == 4 else sent).append((a, j, dst, copy))
    for a, (src, dst) in enumerate(slices):
        for j in range(1, n):
            p = (me + j) % n
            copy = pltpu.make_async_remote_copy(
                src_ref=src.at[my_half, columns(p)],
                dst_ref=dst.at[me, my_half],
                send_sem=send.at[a, j],
                recv_sem=recv.at[a, j],
                device_id=(p, blk),
                device_id_type=MESH,
            )
            copy.start()
            sliced.append((a, j, dst, copy))
    for a, (src, dst) in enumerate(slices):
        copy = pltpu.make_async_copy(src.at[:, columns(me)], dst.at[me], own.at[a])
        copy.start()
        local.append(copy)
    for a, (src, dst) in enumerate(wholes):
        copy = pltpu.make_async_copy(src, dst.at[me], own.at[n_slices + a])
        copy.start()
        local.append(copy)
    forwards = []
    for a, j, dst, copy in passed:
        copy.wait_recv()
        owner, target = (across, along) if j == 1 else (along, across)
        landed = dst.at[owner, pl.ds((j - 1) * half, half)]
        forward = pltpu.make_async_remote_copy(
            src_ref=landed,
            dst_ref=landed,
            send_sem=fsend.at[n_slices + a, j],
            recv_sem=frecv.at[n_slices + a, j],
            device_id=(target, blk),
            device_id_type=MESH,
        )
        forward.start()
        forwards.append(forward)
    for a, j, dst, copy in sliced:
        copy.wait_recv()
        landed = dst.at[(me + n - j) % n, my_half]
        forward = pltpu.make_async_remote_copy(
            src_ref=landed,
            dst_ref=landed,
            send_sem=fsend.at[a, j],
            recv_sem=frecv.at[a, j],
            device_id=(me, sibling),
            device_id_type=MESH,
        )
        forward.start()
        forwards.append(forward)
    for _, _, _, copy in sliced + passed:
        copy.wait_send()
    for copy in forwards + [copy for _, _, _, copy in sent] + local:
        copy.wait()


def exchange(n, slices, wholes, order, collective_id, cost, through=False):
    total = len(slices) + len(wholes)
    out_shape = [
        jax.ShapeDtypeStruct((n, x.shape[0], x.shape[1] // n), jnp.bfloat16) for x in slices
    ] + [jax.ShapeDtypeStruct((n,) + x.shape, jnp.bfloat16) for x in wholes]
    if through:
        out_shape.append(jax.ShapeDtypeStruct(slices[0].shape, jnp.bfloat16))
    outs = pl.pallas_call(
        functools.partial(exchange_kernel, n, len(slices), len(wholes), len(order)),
        out_shape=out_shape,
        in_specs=[pl.BlockSpec(memory_space=pl.ANY)] * (total + len(order)),
        out_specs=[pl.BlockSpec(memory_space=pl.ANY)] * len(out_shape),
        input_output_aliases={0: total} if through else {},
        scratch_shapes=[pltpu.SemaphoreType.DMA((total, n))] * 4
        + [pltpu.SemaphoreType.DMA((total,))],
        compiler_params=pltpu.CompilerParams(
            collective_id=collective_id, has_side_effects=True
        ),
        cost_estimate=pl.CostEstimate(flops=0, bytes_accessed=cost, transcendentals=0),
    )(*slices, *wholes, *order)
    return [out.reshape(n * out.shape[1], out.shape[2]) for out in outs[:total]] + list(outs[total:])


def local(n, tokens, expert_ids, route_probs, scale_exps, w_gate, w_up, w_down, out_grad):
    scales = jnp.exp2(scale_exps.astype(jnp.float32))
    combine = jnp.sum(jnp.where(expert_ids == 0, route_probs, jnp.zeros_like(route_probs)), axis=1)[
        :, None
    ]
    gathered = lax.all_gather(tokens, "blk", axis=0, tiled=True)
    gate_pre = jnp.dot(gathered, w_gate, preferred_element_type=jnp.float32) * scales[0]
    up_pre = jnp.dot(gathered, w_up, preferred_element_type=jnp.float32) * scales[1]
    sigmoid_gate = jax.nn.sigmoid(gate_pre)
    hidden = (gate_pre * sigmoid_gate * up_pre).astype(jnp.bfloat16)
    out_part = (jnp.dot(hidden, w_down, preferred_element_type=jnp.float32) * scales[2]).astype(
        jnp.bfloat16
    )
    scaled = (combine * out_grad.astype(jnp.float32)).astype(jnp.bfloat16)
    scaled_all = lax.all_gather(scaled, "blk", axis=0, tiled=True)
    scaled_slice, scaled_all = exchange(n, [scaled_all], [], [], 1, 45_000_000, through=True)
    d_hidden = contract_cols(scaled_all, w_down) * scales[2]
    d_gate = (d_hidden * up_pre * sigmoid_gate * (1.0 + gate_pre * (1.0 - sigmoid_gate))).astype(
        jnp.bfloat16
    )
    d_up = (d_hidden * gate_pre * sigmoid_gate).astype(jnp.bfloat16)
    in_part = (
        contract_cols(d_gate, w_gate) * scales[0] + contract_cols(d_up, w_up) * scales[1]
    ).astype(jnp.bfloat16)
    expert_out = lax.psum_scatter(out_part, "blk", scatter_dimension=0, tiled=True)
    mixed = (combine * expert_out.astype(jnp.float32)).astype(jnp.bfloat16)
    input_grad = lax.psum_scatter(in_part, "blk", scatter_dimension=0, tiled=True)
    tokens_slice, hidden_all, d_gate_all, d_up_all = exchange(
        n, [gathered], [hidden, d_gate, d_up], [out_part, in_part, scaled_slice], 0, 300_000_000
    )
    grad_gate = contract_rows(tokens_slice, d_gate_all) * scales[0]
    grad_up = contract_rows(tokens_slice, d_up_all) * scales[1]
    grad_down = contract_rows(hidden_all, scaled_slice) * scales[2]
    return (
        mixed,
        input_grad,
        grad_gate.astype(jnp.bfloat16),
        grad_up.astype(jnp.bfloat16),
        grad_down.astype(jnp.bfloat16),
    )


def solution(mesh):
    return jax.shard_map(
        functools.partial(local, mesh.shape["dp"]),
        mesh=mesh,
        in_specs=(
            P(("dp", "blk"), None),
            P(("dp", "blk"), None),
            P(("dp", "blk"), None),
            P(),
            P(None, "blk"),
            P(None, "blk"),
            P("blk", None),
            P(("dp", "blk"), None),
        ),
        out_specs=(
            P(("dp", "blk"), None),
            P(("dp", "blk"), None),
            P("dp", "blk"),
            P("dp", "blk"),
            P("blk", "dp"),
        ),
        check_vma=False,
    )
```
